32 devices in a mesh: seq: 8 (over z, y), head: 4 (over x, core).
Axes of the slice: x: 2, y: 2, z: 4, core: 2. Of those that a mesh axis runs over, the one named last changes fastest.
Arguments:
- tokens: bfloat16 [4096, 2048], P('seq'), may hold values from -24 to 24
- w_query: bfloat16 [2048, 2048], P(None, 'head'), may hold values from -0.125 to 0.125
- w_key: bfloat16 [2048, 2048], P(None, 'head'), may hold values from -0.125 to 0.125
- w_value: bfloat16 [2048, 2048], P(None, 'head'), may hold values from -0.125 to 0.125
- w_out: bfloat16 [2048, 2048], P('head'), may hold values from -0.125 to 0.125
- shared_gate: bfloat16 [2048, 1024], P(None, 'head'), may hold values from -0.125 to 0.125
- shared_up: bfloat16 [2048, 1024], P(None, 'head'), may hold values from -0.125 to 0.125
- shared_down: bfloat16 [1024, 2048], P('head'), may hold values from -0.1875 to 0.1875
- expert_gate: bfloat16 [64, 2048, 1024], P('seq', None, 'head'), may hold values from -0.125 to 0.125
- expert_up: bfloat16 [64, 2048, 1024], P('seq', None, 'head'), may hold values from -0.125 to 0.125
- expert_down: bfloat16 [64, 1024, 2048], P('seq', 'head'), may hold values from -0.1875 to 0.1875
- expert_ids: int32 [4096, 1], P('seq'), may hold values from 0 to 63; in each aligned block of 512 rows (0 to 511, 512 to 1023, ...) at most 16 rows name the same one
Outputs:
- output: bfloat16 [4096, 2048], P('seq', 'head')
The draws below stay inside these ranges and needn't reach their ends.
Inputs may be any that keep to these rules, and one draw needn't show every extreme that they name: `expert_ids`: among the 512 tokens of one index of seq (aligned blocks of the sequence) at most 16 name the same expert, and in some block of every draw one expert is named by exactly 16 tokens.
All inputs are finite; a program needn't handle non-finite values.
Results may differ from the reference program's by a relative error of at most 0.015.
Values may be sent and summed in bfloat16 or wider, within the bound.
No kernel may reach another device: no remote copies, remote signals or barrier semaphores. Data moves between devices by JAX's collectives and lax.ppermute only.
A program may use at most 128 MiB of HBM per device.

```python
import math
import jax
import jax.numpy as jnp
import numpy as np
from jax import lax

D = 2048
H = 16
HD = 128
SH = 1024
FF = 1024
EXPERTS = 64
TOK_DEV = 512
CAP = 16
TOKENS = 4096
N_SEQ = 8
N_HEAD = 4


def draw_tokens(key, part):
    column_key, row_key, value_key, common_key = jax.random.split(jax.random.fold_in(key, 17), 4)
    columns = jnp.arange(D, dtype=jnp.float32) / D
    column_scale = 0.12 * jnp.exp(columns * math.log(5.0) + jax.random.uniform(column_key, (D,), jnp.float32, 0.0, math.log(2.0)))
    block_count = TOKENS // TOK_DEV
    row_scale = jnp.exp(jax.random.uniform(row_key, (TOKENS, 1), jnp.float32, 0.0, math.log(2.0)))
    values = jnp.clip(jax.random.normal(value_key, (TOKENS, D), jnp.float32), -3.0, 3.0)
    common = jnp.clip(jax.random.normal(common_key, (block_count, 1, D), jnp.float32), -3.0, 3.0)
    values = (values.reshape(block_count, TOK_DEV, D) + common).reshape(TOKENS, D)
    return (values * row_scale * column_scale[None, :]).astype(jnp.bfloat16)


def levels(key, shape, cuts, smallest, largest):
    def one(axis_at, blocks):
        draws = jax.random.uniform(jax.random.fold_in(jax.random.fold_in(key, 6), axis_at), (blocks,), jnp.float32, smallest / len(cuts), largest / len(cuts))
        return jnp.repeat(jnp.exp(draws), shape[axis_at] // blocks).reshape((-1,) + (1,) * (len(shape) - axis_at - 1))

    level = one(*cuts[0])
    for cut in cuts[1:]:
        level = level * one(*cut)
    return level


def deal_out(stream_key, own, number, rows, amount, top, limit, lean):
    ranking = jax.random.permutation(stream_key, amount)
    crowded, usual = portions_of(amount, rows * top, limit, lean, True), portions_of(amount, rows * top, limit, lean, False)
    places = jnp.arange(amount)

    def named(tallies, offset_by):
        used = int((tallies > 0).sum())
        fixed = max(1, used // 4)
        passed = fixed + (places - fixed + offset_by * (used - fixed)) % max(1, amount - fixed)
        return jnp.zeros((amount,), jnp.int32).at[ranking[jnp.where(places < fixed, places, passed)]].set(jnp.asarray(tallies, jnp.int32))

    tallies = jnp.where(number % 4 == 0, named(crowded, number // 4), named(usual, number - number // 4 - 1))
    mixed = jax.random.permutation(jax.random.fold_in(own, 3), amount)
    source_of, taker = mixed[0:amount // 2 * 2:2], mixed[1:amount // 2 * 2:2]
    room = jnp.minimum(tallies[source_of] - 1, limit - tallies[taker]) // 2
    room = jnp.where((source_of == ranking[0]) | (taker == ranking[0]) | (tallies[taker] == 0), 0, jnp.maximum(room, 0))
    passed = jax.random.randint(jax.random.fold_in(own, 4), (amount // 2,), 0, 1 << 20) % (room + 1)
    tallies = tallies.at[source_of].add(-passed).at[taker].add(passed)
    members = jnp.searchsorted(jnp.cumsum(tallies), jnp.arange(rows * top), side="right").astype(jnp.int32)
    grid = members.reshape(top, rows).T
    grid = grid[jax.random.permutation(jax.random.fold_in(own, 1), rows)]
    offset_by = jax.random.randint(jax.random.fold_in(own, 2), (rows, 1), 0, top)
    return jnp.take_along_axis(grid, (jnp.arange(top)[None, :] + offset_by) % top, axis=1)


def portions_of(count, total, most, skew, full):
    portions = [(1 << 20) // math.isqrt(grade ** skew) + 1 for grade in range(1, count + 1)]
    largest = most if full else min(most, max(-(-total // count), total * portions[0] // sum(portions)))
    least = 1 if total - largest >= count - 1 else 0
    given, rest = [largest] + [least] * (count - 1), total - largest - least * (count - 1)
    while rest > 0:
        movable = [i for i in range(1, count) if given[i] < largest] or [i for i in range(1, count) if given[i] < most]
        whole, left = sum([portions[i] for i in movable]), rest
        for i in movable:
            addition = min(most - given[i], max(1, left * portions[i] // whole), rest)
            given[i] = given[i] + addition
            rest = rest - addition
    return np.array(given)


def bell_draw(stream_key, extent, spread, bound, shards=(), kind=jnp.bfloat16):
    factor_of = levels(stream_key, extent, shards, -0.22, 0.18) if shards else 1.0
    values = jax.random.normal(stream_key, extent, jnp.float32) * spread * factor_of
    return jnp.minimum(jnp.maximum(values, -bound), bound).astype(kind)


def setup_inputs(seed: int = 0) -> dict:
    splits = jax.random.split(jax.random.key(seed), 13)
    tokens = draw_tokens(jax.random.fold_in(splits[12], 71), 0)
    w_query = bell_draw(splits[1], (D, H * HD), D ** -0.5, 0.125, ((1, 4),))
    w_key = bell_draw(splits[2], (D, H * HD), D ** -0.5, 0.125, ((1, 4),))
    w_value = bell_draw(splits[3], (D, H * HD), D ** -0.5, 0.125, ((1, 4),))
    w_out = bell_draw(splits[4], (H * HD, D), (H * HD) ** -0.5, 0.125, ((0, 4),))
    shared_gate = bell_draw(splits[5], (D, SH), D ** -0.5, 0.125, ((1, 4),))
    shared_up = bell_draw(splits[6], (D, SH), D ** -0.5, 0.125, ((1, 4),))
    shared_down = bell_draw(splits[7], (SH, D), SH ** -0.5, 0.1875, ((0, 4),))
    expert_gate = bell_draw(splits[8], (EXPERTS, D, FF), D ** -0.5, 0.125, ((0, 8), (2, 4)))
    expert_up = bell_draw(splits[9], (EXPERTS, D, FF), D ** -0.5, 0.125, ((0, 8), (2, 4)))
    expert_down = bell_draw(splits[10], (EXPERTS, FF, D), FF ** -0.5, 0.1875, ((0, 8), (1, 4)))
    expert_ids_keys = jax.random.split(jax.random.fold_in(splits[11], 1), TOKENS // TOK_DEV)
    expert_ids_turns = jax.random.permutation(jax.random.fold_in(splits[11], 3), TOKENS // TOK_DEV)
    expert_ids = jax.vmap(lambda own, number: deal_out(jax.random.fold_in(splits[11], 2), own, number, TOK_DEV, EXPERTS, 1, CAP, 2))(expert_ids_keys, expert_ids_turns).reshape((TOKENS, 1))
    return {"tokens": tokens, "w_query": w_query, "w_key": w_key, "w_value": w_value, "w_out": w_out, "shared_gate": shared_gate, "shared_up": shared_up, "shared_down": shared_down, "expert_gate": expert_gate, "expert_up": expert_up, "expert_down": expert_down, "expert_ids": expert_ids}


def rms_rows(values):
    return values * lax.rsqrt(lax.optimization_barrier(jnp.mean(values * values, axis=-1, keepdims=True)) + 1e-06)

def reference(tokens, w_query, w_key, w_value, w_out, shared_gate, shared_up, shared_down, expert_gate, expert_up, expert_down, expert_ids):
    highest = lax.Precision.HIGHEST
    inputs = tokens.astype(jnp.float32)
    normed_input = rms_rows(inputs).astype(jnp.bfloat16)
    query_rows = jnp.dot(normed_input, w_query, preferred_element_type=jnp.float32).astype(jnp.bfloat16)
    key_rows = jnp.dot(normed_input, w_key, preferred_element_type=jnp.float32).astype(jnp.bfloat16)
    value_rows = jnp.dot(normed_input, w_value, preferred_element_type=jnp.float32).astype(jnp.bfloat16)
    block_count = TOKENS // TOK_DEV

    def split_blocks(array):
        return array.astype(jnp.float32).reshape(block_count, TOK_DEV, H, HD)
    causal = jnp.arange(TOK_DEV)[:, None] >= jnp.arange(TOK_DEV)[None, :]

    def advance(states, block_in):
        query_block, key_block, value_block = block_in
        scores = jnp.einsum('thd,shd->hts', query_block, key_block, precision=highest)
        scores = jnp.where(causal[None], scores, 0.0)
        within = jnp.einsum('hts,shd->thd', scores, value_block, precision=highest)
        before = jnp.einsum('thd,hde->the', query_block, states, precision=highest)
        states = states + jnp.einsum('thd,the->hde', key_block, value_block, precision=highest)
        return (states, within + before)
    _, attended = lax.scan(advance, jnp.zeros((H, HD, HD), jnp.float32), (split_blocks(query_rows), split_blocks(key_rows), split_blocks(value_rows)))
    attended = attended.reshape(TOKENS, H, HD)
    head_normed = rms_rows(attended).reshape(TOKENS, H * HD).astype(jnp.bfloat16)
    group_cols = H * HD // N_HEAD
    attn_sum = jnp.zeros((TOKENS, D), jnp.float32)
    for group in range(N_HEAD):
        head_term = jnp.dot(head_normed[:, group * group_cols:(group + 1) * group_cols], w_out[group * group_cols:(group + 1) * group_cols], preferred_element_type=jnp.float32).astype(jnp.bfloat16)
        attn_sum = attn_sum + lax.optimization_barrier(head_term).astype(jnp.float32)
    residual = inputs + attn_sum
    normed_mid = rms_rows(residual).astype(jnp.bfloat16)
    shared_hidden = (jax.nn.silu(jnp.dot(normed_mid, shared_gate, preferred_element_type=jnp.float32)) * jnp.dot(normed_mid, shared_up, preferred_element_type=jnp.float32)).astype(jnp.bfloat16)
    expert_of = expert_ids[:, 0].astype(jnp.int32)
    onehot = (expert_of.reshape(N_SEQ, TOK_DEV, 1) == jnp.arange(EXPERTS, dtype=jnp.int32)[None, None, :]).astype(jnp.int32)
    slot_rank = (lax.optimization_barrier(jnp.sum(jnp.cumsum(onehot, axis=1) * onehot, axis=2)).reshape(TOKENS) - 1).astype(jnp.int32)
    block_index = (jnp.arange(TOKENS, dtype=jnp.int32) // TOK_DEV).astype(jnp.int32)
    position = (expert_of * (N_SEQ * CAP) + block_index * CAP + slot_rank).astype(jnp.int32)
    buffer_rows = EXPERTS * N_SEQ * CAP
    buffer = jnp.zeros((buffer_rows, D), jnp.bfloat16).at[position].set(normed_mid)
    buffer = buffer.reshape(EXPERTS, N_SEQ * CAP, D)
    routed_hidden = lax.map(lambda operands: (jax.nn.silu(jnp.dot(operands[0], operands[1], preferred_element_type=jnp.float32)) * jnp.dot(operands[0], operands[2], preferred_element_type=jnp.float32)).astype(jnp.bfloat16), (buffer, expert_gate, expert_up))
    expert_cols = FF // N_HEAD
    shared_cols = SH // N_HEAD
    routed_sum = jnp.zeros((TOKENS, D), jnp.float32)
    shared_sum = jnp.zeros((TOKENS, D), jnp.float32)
    for group in range(N_HEAD):
        low = group * expert_cols
        routed_term = lax.map(lambda operands: jnp.dot(operands[0][:, low:low + expert_cols], operands[1][low:low + expert_cols], preferred_element_type=jnp.float32).astype(jnp.bfloat16), (routed_hidden, expert_down))
        routed_term = routed_term.reshape(buffer_rows, D)[position]
        routed_sum = routed_sum + lax.optimization_barrier(routed_term).astype(jnp.float32)
        shared_term = jnp.dot(shared_hidden[:, group * shared_cols:(group + 1) * shared_cols], shared_down[group * shared_cols:(group + 1) * shared_cols], preferred_element_type=jnp.float32).astype(jnp.bfloat16)
        shared_sum = shared_sum + lax.optimization_barrier(shared_term).astype(jnp.float32)
    routed_total = routed_sum.astype(jnp.bfloat16)
    routed_back = lax.optimization_barrier(routed_total).astype(jnp.float32)
    return (residual + shared_sum + routed_back).astype(jnp.bfloat16)
```

```python
import jax
import jax.numpy as jnp
from jax import lax
from jax.sharding import PartitionSpec as P

HD = 128
CAP = 16
EPS = 1e-06
CHUNKS = 2
BF16 = jnp.bfloat16
F32 = jnp.float32


def bits_of(size):
    return size.bit_length() - 1


def bit_reverse(value, size):
    out = value * 0
    for bit in range(bits_of(size)):
        out = out | (((value >> bit) & 1) << (bits_of(size) - 1 - bit))
    return out


def swap(array, axis, mask):
    size = lax.axis_size(axis)
    return lax.ppermute(array, axis, [(i, i ^ mask) for i in range(size)])


def exclusive_sum(state):
    size, mine = lax.axis_size("seq"), lax.axis_index("seq")
    total, before = state, jnp.zeros_like(state)
    for bit in range(bits_of(size)):
        got = swap(total.astype(BF16), "seq", 1 << bit).astype(F32)
        before = before + jnp.where((mine >> bit) & 1 == 1, got, 0.0)
        total = total + got
    return before


def halve(partial, dim):
    for bit in range(bits_of(lax.axis_size("head"))):
        half = partial.shape[dim] // 2
        keep = lax.slice_in_dim(partial, 0, half, axis=dim)
        send = lax.slice_in_dim(partial, half, 2 * half, axis=dim).astype(BF16)
        partial = keep + swap(send, "head", 1 << bit).astype(F32)
    return partial


def double(array, dim):
    for bit in reversed(range(bits_of(lax.axis_size("head")))):
        array = jnp.concatenate([array, swap(array, "head", 1 << bit)], axis=dim)
    return array


def exchange(blocks):
    parts = [blocks[0]]
    for k in range(1, lax.axis_size("seq")):
        parts.append(swap(blocks[k], "seq", k))
    return jnp.stack(parts)


def one_hot(index, size):
    return (jnp.arange(size, dtype=jnp.int32)[:, None] == index[None, :]).astype(BF16)


def shards(
    tokens,
    w_query,
    w_key,
    w_value,
    w_out,
    shared_gate,
    shared_up,
    shared_down,
    expert_gate,
    expert_up,
    expert_down,
    expert_ids,
):
    n_seq, n_head = lax.axis_size("seq"), lax.axis_size("head")
    mine, head = lax.axis_index("seq"), lax.axis_index("head")
    rows, width = tokens.shape
    heads_here = w_query.shape[1] // HD
    experts_here = expert_gate.shape[0]
    part = rows // n_head
    cols = width // n_head
    slots = -(-CAP // n_head)
    chunks = min(CHUNKS, experts_here)
    group = experts_here // chunks

    ids = expert_ids[:, 0]
    order = jnp.arange(rows, dtype=jnp.int32)
    start = jnp.sum((ids[None, :] < ids[:, None]).astype(jnp.int32), axis=1)
    earlier = (ids[None, :] == ids[:, None]) & (order[None, :] < order[:, None])
    rank = jnp.sum(earlier.astype(jnp.int32), axis=1)
    place = start + rank
    quarter = place % n_head
    rel = bit_reverse(quarter ^ head, n_head)
    row = rel * part + place // n_head
    here = order[:, None] == row[None, :]
    deal = here.astype(BF16)
    came_from = jnp.sum(jnp.where(here, order[None, :], 0), axis=1)
    slot = rank // n_head
    owner = (ids // experts_here) ^ mine
    local = ids % experts_here
    cell = (((local // group) * n_seq + owner) * group + local % group) * slots + slot
    own_cell = jnp.sum(jnp.where(here[:part], cell[None, :], 0), axis=1)
    cells = chunks * n_seq * group * slots
    pack = one_hot(own_cell, cells).reshape(chunks, cells // chunks, part)
    back_row = (
        (((local // group) * n_seq + owner) * group + local % group) * n_head + quarter
    ) * slots + slot
    back_rows = cells * n_head
    unpack = (back_row[:, None] == jnp.arange(back_rows, dtype=jnp.int32)[None, :]).astype(BF16)

    block = n_head * group * slots
    at = jnp.arange(block, dtype=jnp.int32)
    at_head = bit_reverse(at // (group * slots), n_head) ^ head
    at_expert = (at // slots) % group
    regroup = one_hot((at_expert * n_head + at_head) * slots + at % slots, block)

    down = jnp.concatenate(
        [
            lax.dynamic_slice_in_dim(
                expert_down, (bit_reverse(i, n_head) ^ head) * cols, cols, 2
            )
            for i in range(n_head)
        ],
        axis=2,
    )
    shared_out = jnp.concatenate(
        [
            lax.dynamic_slice_in_dim(
                shared_down, (bit_reverse(i, n_head) ^ head) * cols, cols, 1
            )
            for i in range(n_head)
        ],
        axis=1,
    )

    inputs = tokens.astype(F32)
    scale = lax.rsqrt(jnp.mean(inputs * inputs, axis=-1, keepdims=True) + EPS)

    def project(weights):
        return (jnp.dot(tokens, weights, preferred_element_type=F32) * scale).astype(BF16)

    key_rows = project(w_key).reshape(rows, heads_here, HD)
    value_rows = project(w_value).reshape(rows, heads_here, HD)
    state = jnp.einsum("thd,the->hde", key_rows, value_rows, preferred_element_type=F32)
    carried = exclusive_sum(state).astype(BF16)
    query_rows = jnp.dot(deal, project(w_query), preferred_element_type=F32)
    query_rows = query_rows.astype(BF16).reshape(rows, heads_here, HD)
    scores = jnp.einsum("thd,shd->hts", query_rows, key_rows, preferred_element_type=F32)
    causal = came_from[:, None] >= order[None, :]
    scores = jnp.where(causal[None], scores, 0.0).astype(BF16)
    attended = jnp.einsum("hts,shd->thd", scores, value_rows, preferred_element_type=F32)
    attended = attended + jnp.einsum(
        "thd,hde->the", query_rows, carried, preferred_element_type=F32
    )
    attended = attended * lax.rsqrt(jnp.mean(attended * attended, axis=-1, keepdims=True) + EPS)
    head_normed = attended.astype(BF16).reshape(rows, heads_here * HD)
    head_term = jnp.dot(head_normed, w_out, preferred_element_type=F32)
    own_tokens = jnp.dot(deal[:part], tokens, preferred_element_type=F32)
    residual = (own_tokens + halve(head_term, 0)).astype(BF16)

    returned = []
    for c in range(chunks):
        outgoing = jnp.dot(pack[c], residual, preferred_element_type=F32).astype(BF16)
        arrived = exchange(outgoing.reshape(n_seq, group * slots, width))
        arrived = double(arrived, 1)
        arrived = jnp.einsum(
            "krq,kqd->krd",
            jnp.broadcast_to(regroup[None], (n_seq, block, block)),
            arrived,
            preferred_element_type=F32,
        ).astype(BF16)
        values = arrived.astype(F32)
        norm = lax.rsqrt(jnp.mean(values * values, axis=-1, keepdims=True) + EPS)
        sorted_rows = arrived.reshape(n_seq, group, n_head * slots, width)
        norm_rows = norm.reshape(n_seq, group, n_head * slots, 1)
        span = slice(c * group, (c + 1) * group)

        def gated(gate, up, by):
            return (jax.nn.silu(gate * by) * (up * by)).astype(BF16)

        hidden = gated(
            jnp.einsum(
                "kecd,edf->kecf", sorted_rows, expert_gate[span], preferred_element_type=F32
            ),
            jnp.einsum("kecd,edf->kecf", sorted_rows, expert_up[span], preferred_element_type=F32),
            norm_rows,
        )
        flat = arrived.reshape(n_seq * block, width)
        shared = gated(
            jnp.dot(flat, shared_gate, preferred_element_type=F32),
            jnp.dot(flat, shared_up, preferred_element_type=F32),
            norm.reshape(n_seq * block, 1),
        )
        total = jnp.einsum("kecf,efd->kecd", hidden, down[span], preferred_element_type=F32)
        total = total.reshape(n_seq * block, width)
        total = total + jnp.dot(shared, shared_out, preferred_element_type=F32)
        total = halve(total, 1)
        total = total + lax.dynamic_slice_in_dim(flat, head * cols, cols, 1).astype(F32)
        back = exchange(total.astype(BF16).reshape(n_seq, block, cols))
        returned.append(back.reshape(n_seq * block, cols))
    result = jnp.dot(unpack, jnp.concatenate(returned), preferred_element_type=F32)
    return result.astype(BF16)


def solution(mesh):
    return jax.shard_map(
        shards,
        mesh=mesh,
        in_specs=(
            P("seq", None),
            P(None, "head"),
            P(None, "head"),
            P(None, "head"),
            P("head", None),
            P(None, "head"),
            P(None, "head"),
            P("head", None),
            P("seq", None, "head"),
            P("seq", None, "head"),
            P("seq", "head", None),
            P("seq", None),
        ),
        out_specs=P("seq", "head"),
        check_vma=False,
    )
```

```python
import functools

import jax
import jax.numpy as jnp
from jax import lax
from jax.experimental import pallas as pl
from jax.experimental.pallas import tpu as pltpu
from jax.sharding import PartitionSpec as P

HD = 128
CAP = 16
EPS = 1e-06
CHUNKS = 2
SCOPED = 24 * 2**20
BF16 = jnp.bfloat16
F32 = jnp.float32


def bits_of(size):
    return size.bit_length() - 1


def bit_reverse(value, size):
    out = value * 0
    for bit in range(bits_of(size)):
        out = out | (((value >> bit) & 1) << (bits_of(size) - 1 - bit))
    return out


def swap(array, axis, mask):
    size = lax.axis_size(axis)
    return lax.ppermute(array, axis, [(i, i ^ mask) for i in range(size)])


def exclusive_sum(state):
    size, mine = lax.axis_size("seq"), lax.axis_index("seq")
    total, before = state, jnp.zeros_like(state)
    for bit in range(bits_of(size)):
        got = swap(total.astype(BF16), "seq", 1 << bit).astype(F32)
        before = before + jnp.where((mine >> bit) & 1 == 1, got, 0.0)
        total = total + got
    return before


def fold(keep, send):
    partial = keep + swap(send, "head", 1).astype(F32)
    for bit in range(1, bits_of(lax.axis_size("head"))):
        half = partial.shape[0] // 2
        sent = swap(partial[half:].astype(BF16), "head", 1 << bit)
        partial = partial[:half] + sent.astype(F32)
    return partial


def fold_columns(own, near, far):
    size = lax.axis_size("head")
    cols = own.shape[-1]
    step = -(-far.shape[0] // 4)
    got = [swap(far[at : at + step], "head", 1) for at in range(0, far.shape[0], step)]
    got = jnp.concatenate(got).astype(F32)
    rest = near.astype(F32) + got[..., cols:]
    own = own + got[..., :cols]
    for bit in range(1, bits_of(size)):
        half = (size >> bit) // 2
        sent = swap(rest[..., (half - 1) * cols :].astype(BF16), "head", 1 << bit).astype(F32)
        own = own + sent[..., :cols]
        rest = rest[..., : (half - 1) * cols] + sent[..., cols:]
    return own


def gather(array, done):
    arrays = [array]
    for bit in reversed(range(bits_of(lax.axis_size("head")))):
        if bit == 0 and done is not None:
            *arrays, _ = lax.optimization_barrier((*arrays, done))
        arrays = arrays + [swap(one, "head", 1 << bit) for one in arrays]
    return arrays


def exchange(blocks):
    parts = [blocks[0]]
    for k in range(1, lax.axis_size("seq")):
        parts.append(swap(blocks[k], "seq", k))
    return jnp.stack(parts)


def one_hot(index, size):
    return (jnp.arange(size, dtype=jnp.int32)[:, None] == index[None, :]).astype(BF16)


def dot(a, b):
    return jnp.dot(a, b, preferred_element_type=F32)


def attention_out_kernel(query, carried, within, w_out, keep, send):
    normed = []
    for i in range(carried.shape[0]):
        span = slice(i * HD, (i + 1) * HD)
        value = within[:, span] + dot(query[:, span], carried[i])
        scale = lax.rsqrt(jnp.mean(value * value, axis=-1, keepdims=True) + EPS)
        normed.append((value * scale).astype(BF16))
    normed = jnp.concatenate(normed, axis=1)
    half = keep.shape[0]
    send[...] = dot(normed[half:], w_out[...]).astype(send.dtype)
    keep[...] = dot(normed[:half], w_out[...])


def attention_out(query, carried, within, w_out):
    rows, width = query.shape[0], w_out.shape[1]
    whole = pl.BlockSpec(memory_space=pltpu.VMEM)
    return pl.pallas_call(
        attention_out_kernel,
        out_shape=(
            jax.ShapeDtypeStruct((rows // 2, width), F32),
            jax.ShapeDtypeStruct((rows // 2, width), BF16),
        ),
        in_specs=[whole] * 4,
        out_specs=(whole, whole),
        cost_estimate=pl.CostEstimate(
            flops=2 * rows * query.shape[1] * (width + HD),
            transcendentals=rows,
            bytes_accessed=8 * rows * width,
        ),
        compiler_params=pltpu.CompilerParams(vmem_limit_bytes=SCOPED),
    )(query, carried, within, w_out)


def expert_kernel(n_head, n_seq, first, group, head, regroup, *refs):
    pieces = refs[:n_head]
    weights = refs[n_head : n_head + 3]
    shared_gate, shared_up, shared_down = refs[n_head + 3 : n_head + 6]
    own, near, far, held, scales = refs[n_head + 6 : n_head + 11]
    gate, up, down, sems = refs[n_head + 11 :]
    copies = {
        (i, e): pltpu.make_async_copy(weights[i].at[first + e], kept.at[e], sems.at[i, e])
        for e in range(group)
        for i, kept in enumerate((gate, up, down))
    }
    for i, e in sorted(copies, key=lambda at: (at[0] == 2, at[1], at[0])):
        copies[i, e].start()
    count = held.shape[0] // group
    size = pieces[0].shape[0]
    cols = own.shape[-1]

    for e in range(group):
        span = slice(e * count, (e + 1) * count)
        value = dot(regroup[span, :size], pieces[0][...])
        for i in range(1, n_head):
            value += dot(regroup[span, i * size : (i + 1) * size], pieces[i][...])
        held[span, :] = value.astype(BF16)
        scale = lax.rsqrt(jnp.mean(value * value, axis=-1, keepdims=True) + EPS)
        scales[span, :] = jnp.broadcast_to(scale, (count, scales.shape[1]))

    def hidden(rows, scale, gate_weight, up_weight):
        value = dot(rows, gate_weight) * scale
        return (value / (1.0 + jnp.exp(-value)) * (dot(rows, up_weight) * scale)).astype(BF16)

    shared = hidden(held[...], scales[:, :1], shared_gate[...], shared_up[...])
    routed = []
    for e in range(group):
        span = slice(e * count, (e + 1) * count)
        copies[0, e].wait()
        copies[1, e].wait()
        routed.append(hidden(held[span, :], scales[span, :1], gate[e], up[e]))
    for e in range(group):
        copies[2, e].wait()

    def columns(i):
        at = (bit_reverse(i, n_head) ^ head[0]) * cols
        return pl.ds(pl.multiple_of(at, cols), cols)

    def store(ref, i, lane):
        at = columns(i)
        common = dot(shared, shared_down[:, at])
        for e in range(group):
            span = slice(e * count, (e + 1) * count)
            value = common[span] + dot(routed[e], down[e, :, at])
            if i == 0:
                value += held[span, at].astype(F32)
            value = value.reshape(n_seq, count // n_seq, cols).astype(ref.dtype)
            ref[:, e, :, lane * cols : (lane + 1) * cols] = value

    half = n_head // 2
    for i in range(half, n_head):
        store(far, i, i - half)
    for i in range(1, half):
        store(near, i, i - 1)
    store(own, 0, 0)


def experts(head, regroup, pieces, first, group, weights, n_seq):
    n_head = len(pieces)
    width = pieces[0].shape[1]
    rows = pieces[0].shape[0] * n_head
    cols = width // n_head

    def result(count, dtype):
        return jax.ShapeDtypeStruct((n_seq, group, rows // group // n_seq, count * cols), dtype)

    whole = pl.BlockSpec(memory_space=pltpu.VMEM)
    return pl.pallas_call(
        functools.partial(expert_kernel, n_head, n_seq, first, group),
        out_shape=[result(1, F32), result(n_head // 2 - 1, BF16), result(n_head // 2, BF16)],
        in_specs=[pl.BlockSpec(memory_space=pltpu.SMEM)]
        + [whole] * (1 + n_head)
        + [pl.BlockSpec(memory_space=pl.ANY)] * 3
        + [whole] * 3,
        out_specs=[whole] * 3,
        scratch_shapes=[pltpu.VMEM((rows, width), BF16), pltpu.VMEM((rows, 128), F32)]
        + [pltpu.VMEM((group,) + w.shape[1:], w.dtype) for w in weights[:3]]
        + [pltpu.SemaphoreType.DMA((3, group))],
        cost_estimate=pl.CostEstimate(
            flops=2 * rows * width * (rows + 6 * weights[0].shape[2]),
            transcendentals=rows * weights[0].shape[2],
            bytes_accessed=6 * (group + 1) * width * weights[0].shape[2] + 8 * rows * width,
        ),
        compiler_params=pltpu.CompilerParams(vmem_limit_bytes=SCOPED),
    )(head, regroup, *pieces, *weights)


def shards(
    tokens,
    w_query,
    w_key,
    w_value,
    w_out,
    shared_gate,
    shared_up,
    shared_down,
    expert_gate,
    expert_up,
    expert_down,
    expert_ids,
):
    n_seq, n_head = lax.axis_size("seq"), lax.axis_size("head")
    mine, head = lax.axis_index("seq"), lax.axis_index("head")
    rows, width = tokens.shape
    heads_here = w_query.shape[1] // HD
    experts_here = expert_gate.shape[0]
    part = rows // n_head
    cols = width // n_head
    slots = -(-CAP // n_head)
    chunks = min(CHUNKS, experts_here)
    group = experts_here // chunks

    ids = expert_ids[:, 0]
    order = jnp.arange(rows, dtype=jnp.int32)
    start = jnp.sum((ids[None, :] < ids[:, None]).astype(jnp.int32), axis=1)
    earlier = (ids[None, :] == ids[:, None]) & (order[None, :] < order[:, None])
    rank = jnp.sum(earlier.astype(jnp.int32), axis=1)
    place = start + rank
    quarter = place % n_head
    rel = bit_reverse(quarter ^ head, n_head)
    row = rel * part + place // n_head
    here = order[:, None] == row[None, :]
    deal = here.astype(BF16)
    came_from = jnp.sum(jnp.where(here, order[None, :], 0), axis=1)
    slot = rank // n_head
    owner = (ids // experts_here) ^ mine
    local = ids % experts_here
    cell = (((local // group) * n_seq + owner) * group + local % group) * slots + slot
    own_cell = jnp.sum(jnp.where(here[:part], cell[None, :], 0), axis=1)
    cells = chunks * n_seq * group * slots
    pack = one_hot(own_cell, cells).reshape(chunks, cells // chunks, part)
    back_row = (
        (((local // group) * n_seq + owner) * group + local % group) * n_head + quarter
    ) * slots + slot
    back_rows = cells * n_head
    unpack = (back_row[:, None] == jnp.arange(back_rows, dtype=jnp.int32)[None, :]).astype(BF16)

    chunk_rows = n_head * n_seq * group * slots
    at = jnp.arange(chunk_rows, dtype=jnp.int32)
    at_slot, at_expert = at % slots, (at // slots) % group
    at_seq = (at // (slots * group)) % n_seq
    at_head = bit_reverse(at // (slots * group * n_seq), n_head) ^ head
    regroup = one_hot(
        ((at_expert * n_seq + at_seq) * n_head + at_head) * slots + at_slot, chunk_rows
    )
    head_index = jnp.reshape(head, (1,)).astype(jnp.int32)

    inputs = tokens.astype(F32)
    scale = lax.rsqrt(jnp.mean(inputs * inputs, axis=-1, keepdims=True) + EPS)

    def project(weights):
        return (jnp.dot(tokens, weights, preferred_element_type=F32) * scale).astype(BF16)

    key_rows = project(w_key).reshape(rows, heads_here, HD)
    value_rows = project(w_value).reshape(rows, heads_here, HD)
    state = jnp.einsum("thd,the->hde", key_rows, value_rows, preferred_element_type=F32)
    carried = exclusive_sum(state).astype(BF16)
    query_rows = jnp.dot(deal, project(w_query), preferred_element_type=F32)
    query_rows = query_rows.astype(BF16).reshape(rows, heads_here, HD)
    scores = jnp.einsum("thd,shd->hts", query_rows, key_rows, preferred_element_type=F32)
    causal = came_from[:, None] >= order[None, :]
    scores = jnp.where(causal[None], scores, 0.0).astype(BF16)
    within = jnp.einsum("hts,shd->thd", scores, value_rows, preferred_element_type=F32)
    keep, send = attention_out(
        query_rows.reshape(rows, heads_here * HD),
        carried,
        within.reshape(rows, heads_here * HD),
        w_out,
    )
    own_tokens = jnp.dot(deal[:part], tokens, preferred_element_type=F32)
    residual = (own_tokens + fold(keep, send)).astype(BF16)

    weights = (expert_gate, expert_up, expert_down, shared_gate, shared_up, shared_down)
    returned = []
    arrivals = []
    for c in range(chunks):
        outgoing = jnp.dot(pack[c], residual, preferred_element_type=F32).astype(BF16)
        arrived = exchange(outgoing.reshape(n_seq, group * slots, width))
        arrivals.append(arrived.reshape(n_seq * group * slots, width))
    done = None
    for c in range(chunks):
        pieces = gather(arrivals[c], done)
        own, near, far = experts(head_index, regroup, pieces, c * group, group, weights, n_seq)
        done = own
        total = fold_columns(own, near, far).astype(BF16)
        back = exchange(total.reshape(n_seq, group * n_head * slots, cols))
        returned.append(back.reshape(n_seq * group * n_head * slots, cols))
    result = jnp.dot(unpack, jnp.concatenate(returned), preferred_element_type=F32)
    return result.astype(BF16)


def solution(mesh):
    return jax.shard_map(
        shards,
        mesh=mesh,
        in_specs=(
            P("seq", None),
            P(None, "head"),
            P(None, "head"),
            P(None, "head"),
            P("head", None),
            P(None, "head"),
            P(None, "head"),
            P("head", None),
            P("seq", None, "head"),
            P("seq", None, "head"),
            P("seq", "head", None),
            P("seq", None),
        ),
        out_specs=P("seq", "head"),
        check_vma=False,
    )
```

```python
import functools

import jax
import jax.numpy as jnp
from jax import lax
from jax.experimental import pallas as pl
from jax.experimental.pallas import tpu as pltpu
from jax.sharding import PartitionSpec as P

HD = 128
CAP = 16
EPS = 1e-06
CHUNKS = 2
SCOPED = 40 * 2**20
BF16 = jnp.bfloat16
F32 = jnp.float32


def bits_of(size):
    return size.bit_length() - 1


def bit_reverse(value, size):
    out = value * 0
    for bit in range(bits_of(size)):
        out = out | (((value >> bit) & 1) << (bits_of(size) - 1 - bit))
    return out


def swap(array, axis, mask):
    size = lax.axis_size(axis)
    return lax.ppermute(array, axis, [(i, i ^ mask) for i in range(size)])


def exclusive_sum(state):
    size, mine = lax.axis_size("seq"), lax.axis_index("seq")
    total, before, first = state, jnp.zeros_like(state), None
    for bit in range(bits_of(size)):
        got = swap(total.astype(BF16), "seq", 1 << bit)
        first = got if first is None else first
        got = got.astype(F32)
        before = before + jnp.where((mine >> bit) & 1 == 1, got, 0.0)
        total = total + got
    return before, first


def fold(keep, send):
    partial, got = keep, swap(send, "head", 1)
    for bit in range(1, bits_of(lax.axis_size("head"))):
        half = partial.shape[0] // 2
        late = partial[half:] + got[half:].astype(F32)
        partial = partial[:half] + got[:half].astype(F32)
        got = swap(late.astype(BF16), "head", 1 << bit)
    return partial, got


def pack_kernel(pack, own_tokens, partial, got, out):
    residual = own_tokens[...].astype(F32) + partial[...] + got[...].astype(F32)
    out[...] = dot(pack[...], residual.astype(BF16)).astype(BF16)


def pack_rows(pack, own_tokens, partial, got):
    whole = pl.BlockSpec(memory_space=pltpu.VMEM)
    return pl.pallas_call(
        pack_kernel,
        out_shape=jax.ShapeDtypeStruct((pack.shape[0], got.shape[1]), BF16),
        in_specs=[whole] * 4,
        out_specs=whole,
        compiler_params=pltpu.CompilerParams(vmem_limit_bytes=12 * 2**20),
    )(pack, own_tokens, partial, got)


def fold_columns(own, near, far, earlier):
    size = lax.axis_size("head")
    cols = own.shape[-1]
    step = -(-far.shape[0] // 4)
    got = [swap(far[at : at + step], "head", 1) for at in range(0, far.shape[0], step)]
    got = jnp.concatenate(got).astype(F32)
    rest = near.astype(F32) + got[..., cols:]
    own = own + got[..., :cols]
    if earlier:
        rest, earlier[-1] = lax.optimization_barrier((rest, earlier[-1]))
    for bit in range(1, bits_of(size)):
        half = (size >> bit) // 2
        sent = swap(rest[..., (half - 1) * cols :].astype(BF16), "head", 1 << bit).astype(F32)
        own = own + sent[..., :cols]
        rest = rest[..., : (half - 1) * cols] + sent[..., cols:]
    return own


def gather(array, done):
    arrays = [array]
    for bit in reversed(range(bits_of(lax.axis_size("head")))):
        if bit == 0 and done is not None:
            *arrays, _ = lax.optimization_barrier((*arrays, done))
        arrays = arrays + [swap(one, "head", 1 << bit) for one in arrays]
    return arrays


def unstack(rows, half, chunks, size):
    near = [rows[k * chunks * size : (k + 1) * chunks * size] for k in range(half)]
    at = half * chunks * size
    far = [
        [rows[at + (c * half + k) * size : at + (c * half + k + 1) * size] for k in range(half)]
        for c in range(chunks)
    ]
    return near, far


def one_hot(index, size):
    return (jnp.arange(size, dtype=jnp.int32)[:, None] == index[None, :]).astype(BF16)


def dot(a, b):
    return jnp.dot(a, b, preferred_element_type=F32)


def attention_out_kernel(query, carried, within, w_out, keep, send):
    normed = []
    for i in range(carried.shape[0]):
        span = slice(i * HD, (i + 1) * HD)
        value = within[i] + dot(query[:, span], carried[i])
        scale = lax.rsqrt(jnp.mean(value * value, axis=-1, keepdims=True) + EPS)
        normed.append((value * scale).astype(BF16))
    normed = jnp.concatenate(normed, axis=1)
    half = keep.shape[0]
    send[...] = dot(normed[half:], w_out[...]).astype(send.dtype)
    keep[...] = dot(normed[:half], w_out[...])


def attention_out(query, carried, within, w_out):
    rows, width = query.shape[0], w_out.shape[1]
    whole = pl.BlockSpec(memory_space=pltpu.VMEM)
    return pl.pallas_call(
        attention_out_kernel,
        out_shape=(
            jax.ShapeDtypeStruct((rows // 2, width), F32),
            jax.ShapeDtypeStruct((rows // 2, width), BF16),
        ),
        in_specs=[whole] * 4,
        out_specs=(whole, whole),
        cost_estimate=pl.CostEstimate(
            flops=2 * rows * query.shape[1] * (width + HD),
            transcendentals=rows,
            bytes_accessed=8 * rows * width,
        ),
        compiler_params=pltpu.CompilerParams(vmem_limit_bytes=12 * 2**20),
    )(query, carried, within, w_out)


def expert_kernel(n_head, n_seq, first, group, head, regroup, *refs):
    pieces = refs[:n_head]
    weights = refs[n_head : n_head + 3]
    shared_in = refs[n_head + 3 : n_head + 6]
    own, near, far, held, scales = refs[n_head + 6 : n_head + 11]
    gate, up, down, shared_gate, shared_up, shared_down, sems = refs[n_head + 11 :]
    copies = {
        (i, e): pltpu.make_async_copy(weights[i].at[first + e], kept.at[e], sems.at[i, e])
        for e in range(group)
        for i, kept in enumerate((gate, up, down))
    }
    for i, kept in enumerate((shared_gate, shared_up, shared_down)):
        copies[i, group] = pltpu.make_async_copy(shared_in[i], kept, sems.at[i, group])
    for i, e in sorted(copies, key=lambda at: (at[0] == 2, at[1], at[0])):
        copies[i, e].start()
    count = held.shape[0] // group
    size = pieces[0].shape[0]
    cols = own.shape[-1]

    for e in range(group):
        span = slice(e * count, (e + 1) * count)
        value = dot(regroup[span, :size], pieces[0][...])
        for i in range(1, n_head):
            value += dot(regroup[span, i * size : (i + 1) * size], pieces[i][...])
        held[span, :] = value.astype(BF16)
        scale = lax.rsqrt(jnp.mean(value * value, axis=-1, keepdims=True) + EPS)
        scales[span, :] = jnp.broadcast_to(scale, (count, scales.shape[1]))

    def hidden(rows, scale, gate_weight, up_weight):
        value = dot(rows, gate_weight) * scale
        return (value / (1.0 + jnp.exp(-value)) * (dot(rows, up_weight) * scale)).astype(BF16)

    routed = []
    for e in range(group):
        span = slice(e * count, (e + 1) * count)
        copies[0, e].wait()
        copies[1, e].wait()
        routed.append(hidden(held[span, :], scales[span, :1], gate[e], up[e]))
    copies[0, group].wait()
    copies[1, group].wait()
    shared = hidden(held[...], scales[:, :1], shared_gate[...], shared_up[...])
    for e in range(group + 1):
        copies[2, e].wait()

    def columns(i):
        at = (bit_reverse(i, n_head) ^ head[0]) * cols
        return pl.ds(pl.multiple_of(at, cols), cols)

    def store(ref, i, lane):
        at = columns(i)
        common = dot(shared, shared_down[:, at])
        for e in range(group):
            span = slice(e * count, (e + 1) * count)
            value = common[span] + dot(routed[e], down[e, :, at])
            if i == 0:
                value += held[span, at].astype(F32)
            value = value.reshape(n_seq, count // n_seq, cols).astype(ref.dtype)
            ref[:, e, :, lane * cols : (lane + 1) * cols] = value

    half = n_head // 2
    for i in range(half, n_head):
        store(far, i, i - half)
    for i in range(1, half):
        store(near, i, i - 1)
    store(own, 0, 0)


def experts(head, regroup, pieces, first, group, weights, n_seq):
    n_head = len(pieces)
    width = pieces[0].shape[1]
    rows = pieces[0].shape[0] * n_head
    cols = width // n_head

    def result(count, dtype):
        return jax.ShapeDtypeStruct((n_seq, group, rows // group // n_seq, count * cols), dtype)

    whole = pl.BlockSpec(memory_space=pltpu.VMEM)
    return pl.pallas_call(
        functools.partial(expert_kernel, n_head, n_seq, first, group),
        out_shape=[result(1, F32), result(n_head // 2 - 1, BF16), result(n_head // 2, BF16)],
        in_specs=[pl.BlockSpec(memory_space=pltpu.SMEM)]
        + [whole] * (1 + n_head)
        + [pl.BlockSpec(memory_space=pltpu.HBM)] * 6,
        out_specs=[whole] * 3,
        scratch_shapes=[pltpu.VMEM((rows, width), BF16), pltpu.VMEM((rows, 128), F32)]
        + [pltpu.VMEM((group,) + w.shape[1:], w.dtype) for w in weights[:3]]
        + [pltpu.VMEM(w.shape, w.dtype) for w in weights[3:]]
        + [pltpu.SemaphoreType.DMA((3, group + 1))],
        cost_estimate=pl.CostEstimate(
            flops=2 * rows * width * (rows + 6 * weights[0].shape[2]),
            transcendentals=rows * weights[0].shape[2],
            bytes_accessed=6 * (group + 1) * width * weights[0].shape[2] + 8 * rows * width,
        ),
        compiler_params=pltpu.CompilerParams(vmem_limit_bytes=SCOPED),
    )(head, regroup, *pieces, *weights)


def shards(
    tokens,
    w_query,
    w_key,
    w_value,
    w_out,
    shared_gate,
    shared_up,
    shared_down,
    expert_gate,
    expert_up,
    expert_down,
    expert_ids,
):
    n_seq, n_head = lax.axis_size("seq"), lax.axis_size("head")
    mine, head = lax.axis_index("seq"), lax.axis_index("head")
    rows, width = tokens.shape
    heads_here = w_query.shape[1] // HD
    experts_here = expert_gate.shape[0]
    part = rows // n_head
    cols = width // n_head
    slots = -(-CAP // n_head)
    chunks = min(CHUNKS, experts_here)
    group = experts_here // chunks

    ids = expert_ids[:, 0]
    order = jnp.arange(rows, dtype=jnp.int32)
    start = jnp.sum((ids[None, :] < ids[:, None]).astype(jnp.int32), axis=1)
    earlier = (ids[None, :] == ids[:, None]) & (order[None, :] < order[:, None])
    rank = jnp.sum(earlier.astype(jnp.int32), axis=1)
    place = start + rank
    quarter = place % n_head
    rel = bit_reverse(quarter ^ head, n_head)
    row = rel * part + place // n_head
    here = order[:, None] == row[None, :]
    deal = here.astype(BF16)
    came_from = jnp.sum(jnp.where(here, order[None, :], 0), axis=1)
    slot = rank // n_head
    owner = (ids // experts_here) ^ mine
    local = ids % experts_here
    half = n_seq // 2

    def place_in(inner, size):
        near = (owner * chunks + local // group) * size
        far = (half * chunks + (local // group) * half + owner - half) * size
        return jnp.where(owner < half, near, far) + inner

    sent_rows, back_size = group * slots, group * slots * n_head
    cell = place_in((local % group) * slots + slot, sent_rows)
    own_cell = jnp.sum(jnp.where(here[:part], cell[None, :], 0), axis=1)
    pack = one_hot(own_cell, n_seq * chunks * sent_rows)
    back_row = place_in(((local % group) * n_head + quarter) * slots + slot, back_size)
    unpack = (
        back_row[:, None] == jnp.arange(n_seq * chunks * back_size, dtype=jnp.int32)[None, :]
    ).astype(BF16)

    chunk_rows = n_head * n_seq * group * slots
    at = jnp.arange(chunk_rows, dtype=jnp.int32)
    at_slot, at_expert = at % slots, (at // slots) % group
    at_seq = (at // (slots * group)) % n_seq
    at_head = bit_reverse(at // (slots * group * n_seq), n_head) ^ head
    regroup = one_hot(
        ((at_expert * n_seq + at_seq) * n_head + at_head) * slots + at_slot, chunk_rows
    )
    head_index = jnp.reshape(head, (1,)).astype(jnp.int32)

    inputs = tokens.astype(F32)
    scale = lax.rsqrt(jnp.mean(inputs * inputs, axis=-1, keepdims=True) + EPS)

    def project(weights, scale):
        return (jnp.dot(tokens, weights, preferred_element_type=F32) * scale).astype(BF16)

    key_rows = project(w_key, scale).reshape(rows, heads_here, HD)
    value_rows = project(w_value, scale).reshape(rows, heads_here, HD)
    state = jnp.einsum("thd,the->hde", key_rows, value_rows, preferred_element_type=F32)
    carried, first = exclusive_sum(state)
    carried = carried.astype(BF16)
    scale, _ = lax.optimization_barrier((scale, first))
    query_rows = jnp.dot(deal, project(w_query, scale), preferred_element_type=F32)
    query_rows = query_rows.astype(BF16).reshape(rows, heads_here, HD)
    scores = jnp.einsum("thd,shd->hts", query_rows, key_rows, preferred_element_type=F32)
    causal = came_from[:, None] >= order[None, :]
    scores = jnp.where(causal[None], scores, 0.0).astype(BF16)
    within = jnp.einsum("hts,shd->htd", scores, value_rows, preferred_element_type=F32)
    keep, send = attention_out(
        query_rows.reshape(rows, heads_here * HD),
        carried,
        within,
        w_out,
    )
    own_tokens = dot(deal[:part], tokens).astype(BF16)
    partial, got = fold(keep, send)

    weights = (expert_gate, expert_up, expert_down, shared_gate, shared_up, shared_down)
    outgoing = pack_rows(pack, own_tokens, partial, got)
    near, far = unstack(outgoing, half, chunks, sent_rows)
    near = [near[0]] + [swap(near[k], "seq", k) for k in range(1, half)]
    far = [[swap(far[c][k], "seq", half + k) for k in range(half)] for c in range(chunks)]
    totals = []
    done = None
    for c in range(chunks):
        blocks = [block[c * sent_rows : (c + 1) * sent_rows] for block in near] + far[c]
        pieces = gather(jnp.concatenate(blocks), done)
        own, rest, other = experts(head_index, regroup, pieces, c * group, group, weights, n_seq)
        done = own
        total = fold_columns(own, rest, other, totals).astype(BF16)
        totals.append(total.reshape(n_seq, back_size, cols))
    back = [jnp.concatenate([total[k] for total in totals]) for k in range(half)]
    far = [[swap(total[k], "seq", k) for k in range(half, n_seq)] for total in totals]
    tied = lax.optimization_barrier((*back[1:], *far[0]))
    back = back[:1] + [swap(tied[k], "seq", k + 1) for k in range(half - 1)]
    back = back + list(tied[half - 1 :]) + [one for blocks in far[1:] for one in blocks]
    result = dot(unpack, jnp.concatenate(back))
    return result.astype(BF16)


def solution(mesh):
    return jax.shard_map(
        shards,
        mesh=mesh,
        in_specs=(
            P("seq", None),
            P(None, "head"),
            P(None, "head"),
            P(None, "head"),
            P("head", None),
            P(None, "head"),
            P(None, "head"),
            P("head", None),
            P("seq", None, "head"),
            P("seq", None, "head"),
            P("seq", "head", None),
            P("seq", None),
        ),
        out_specs=P("seq", "head"),
        check_vma=False,
    )
```

```python
import functools

import jax
import jax.numpy as jnp
from jax import lax
from jax.experimental import pallas as pl
from jax.experimental.pallas import tpu as pltpu
from jax.sharding import PartitionSpec as P

HD = 128
CAP = 16
EPS = 1e-06
CHUNKS = 2
SCOPED = 40 * 2**20
BF16 = jnp.bfloat16
F32 = jnp.float32


def bits_of(size):
    return size.bit_length() - 1


def bit_reverse(value, size):
    out = value * 0
    for bit in range(bits_of(size)):
        out = out | (((value >> bit) & 1) << (bits_of(size) - 1 - bit))
    return out


def swap(array, axis, mask):
    size = lax.axis_size(axis)
    return lax.ppermute(array, axis, [(i, i ^ mask) for i in range(size)])


def exclusive_sum(state):
    size, mine = lax.axis_size("seq"), lax.axis_index("seq")
    total, before, first = state, jnp.zeros_like(state), None
    for bit in range(bits_of(size)):
        got = swap(total.astype(BF16), "seq", 1 << bit)
        first = got if first is None else first
        got = got.astype(F32)
        before = before + jnp.where((mine >> bit) & 1 == 1, got, 0.0)
        total = total + got
    return before, first


def fold(keep, send):
    partial, got = keep, swap(send, "head", 1)
    for bit in range(1, bits_of(lax.axis_size("head"))):
        half = partial.shape[0] // 2
        late = partial[half:] + got[half:].astype(F32)
        partial = partial[:half] + got[:half].astype(F32)
        got = swap(late.astype(BF16), "head", 1 << bit)
    return partial, got


def pack_kernel(pack, own_tokens, partial, got, out):
    residual = own_tokens[...].astype(F32) + partial[...] + got[...].astype(F32)
    out[...] = dot(pack[...], residual.astype(BF16)).astype(BF16)


def pack_rows(pack, own_tokens, partial, got):
    whole = pl.BlockSpec(memory_space=pltpu.VMEM)
    return pl.pallas_call(
        pack_kernel,
        out_shape=jax.ShapeDtypeStruct((pack.shape[0], got.shape[1]), BF16),
        in_specs=[whole] * 4,
        out_specs=whole,
        compiler_params=pltpu.CompilerParams(vmem_limit_bytes=12 * 2**20),
    )(pack, own_tokens, partial, got)


def fold_columns(own, near, far, earlier):
    size = lax.axis_size("head")
    cols = own.shape[-1]
    step = -(-far.shape[0] // 4)
    got = [swap(far[at : at + step], "head", 1) for at in range(0, far.shape[0], step)]
    got = jnp.concatenate(got).astype(F32)
    rest = near.astype(F32) + got[..., cols:]
    own = own + got[..., :cols]
    if earlier:
        rest, earlier[-1] = lax.optimization_barrier((rest, earlier[-1]))
    for bit in range(1, bits_of(size)):
        half = (size >> bit) // 2
        sent = swap(rest[..., (half - 1) * cols :].astype(BF16), "head", 1 << bit).astype(F32)
        own = own + sent[..., :cols]
        rest = rest[..., : (half - 1) * cols] + sent[..., cols:]
    return own


def gather(array, done):
    arrays = [array]
    for bit in reversed(range(bits_of(lax.axis_size("head")))):
        if bit == 0 and done is not None:
            *arrays, _ = lax.optimization_barrier((*arrays, done))
        arrays = arrays + [swap(one, "head", 1 << bit) for one in arrays]
    return arrays


def unstack(rows, half, chunks, size):
    near = [rows[k * chunks * size : (k + 1) * chunks * size] for k in range(half)]
    at = half * chunks * size
    far = [
        [rows[at + (c * half + k) * size : at + (c * half + k + 1) * size] for k in range(half)]
        for c in range(chunks)
    ]
    return near, far


def one_hot(index, size):
    return (jnp.arange(size, dtype=jnp.int32)[:, None] == index[None, :]).astype(BF16)


def dot(a, b):
    return jnp.dot(a, b, preferred_element_type=F32)


def attention_out_kernel(query, carried, within, w_out, keep, send):
    normed = []
    for i in range(carried.shape[0]):
        span = slice(i * HD, (i + 1) * HD)
        value = within[i] + dot(query[:, span], carried[i])
        scale = lax.rsqrt(jnp.mean(value * value, axis=-1, keepdims=True) + EPS)
        normed.append((value * scale).astype(BF16))
    normed = jnp.concatenate(normed, axis=1)
    half = keep.shape[0]
    send[...] = dot(normed[half:], w_out[...]).astype(send.dtype)
    keep[...] = dot(normed[:half], w_out[...])


def attention_out(query, carried, within, w_out):
    rows, width = query.shape[0], w_out.shape[1]
    whole = pl.BlockSpec(memory_space=pltpu.VMEM)
    return pl.pallas_call(
        attention_out_kernel,
        out_shape=(
            jax.ShapeDtypeStruct((rows // 2, width), F32),
            jax.ShapeDtypeStruct((rows // 2, width), BF16),
        ),
        in_specs=[whole] * 4,
        out_specs=(whole, whole),
        cost_estimate=pl.CostEstimate(
            flops=2 * rows * query.shape[1] * (width + HD),
            transcendentals=rows,
            bytes_accessed=8 * rows * width,
        ),
        compiler_params=pltpu.CompilerParams(vmem_limit_bytes=12 * 2**20),
    )(query, carried, within, w_out)


def expert_kernel(n_head, n_seq, first, group, head, regroup, *refs):
    pieces = refs[:n_head]
    weights = refs[n_head : n_head + 3]
    shared_in = refs[n_head + 3 : n_head + 6]
    own, near, far, held, scales = refs[n_head + 6 : n_head + 11]
    gate, up, down, shared_gate, shared_up, shared_down, cat, sems = refs[n_head + 11 :]
    copies = {
        (i, e): pltpu.make_async_copy(weights[i].at[first + e], kept.at[e], sems.at[i, e])
        for e in range(group)
        for i, kept in enumerate((gate, up, down))
    }
    for i, kept in enumerate((shared_gate, shared_up, shared_down)):
        copies[i, group] = pltpu.make_async_copy(shared_in[i], kept, sems.at[i, group])
    for i, e in sorted(copies, key=lambda at: (at[0] == 2, at[1], at[0])):
        copies[i, e].start()
    count = held.shape[0] // group
    size = pieces[0].shape[0]
    cols = own.shape[-1]

    for i in range(n_head):
        cat[i * size : (i + 1) * size, :] = pieces[i][...]
    for e in range(group):
        span = slice(e * count, (e + 1) * count)
        value = dot(regroup[span, :], cat[...])
        held[span, :] = value.astype(BF16)
        scale = lax.rsqrt(jnp.mean(value * value, axis=-1, keepdims=True) + EPS)
        scales[span, :] = jnp.broadcast_to(scale, (count, scales.shape[1]))

    def hidden(rows, scale, gate_weight, up_weight):
        value = dot(rows, gate_weight) * scale
        return (value / (1.0 + jnp.exp(-value)) * (dot(rows, up_weight) * scale)).astype(BF16)

    routed = []
    for e in range(group):
        span = slice(e * count, (e + 1) * count)
        copies[0, e].wait()
        copies[1, e].wait()
        routed.append(hidden(held[span, :], scales[span, :1], gate[e], up[e]))
    copies[0, group].wait()
    copies[1, group].wait()
    shared = hidden(held[...], scales[:, :1], shared_gate[...], shared_up[...])
    for e in range(group + 1):
        copies[2, e].wait()

    def columns(i):
        at = (bit_reverse(i, n_head) ^ head[0]) * cols
        return pl.ds(pl.multiple_of(at, cols), cols)

    def store(ref, i, lane):
        at = columns(i)
        common = dot(shared, shared_down[:, at])
        for e in range(group):
            span = slice(e * count, (e + 1) * count)
            value = common[span] + dot(routed[e], down[e, :, at])
            if i == 0:
                value += held[span, at].astype(F32)
            value = value.reshape(n_seq, count // n_seq, cols).astype(ref.dtype)
            ref[:, e, :, lane * cols : (lane + 1) * cols] = value

    half = n_head // 2
    for i in range(half, n_head):
        store(far, i, i - half)
    for i in range(1, half):
        store(near, i, i - 1)
    store(own, 0, 0)


def experts(head, regroup, pieces, first, group, weights, n_seq):
    n_head = len(pieces)
    width = pieces[0].shape[1]
    rows = pieces[0].shape[0] * n_head
    cols = width // n_head

    def result(count, dtype):
        return jax.ShapeDtypeStruct((n_seq, group, rows // group // n_seq, count * cols), dtype)

    whole = pl.BlockSpec(memory_space=pltpu.VMEM)
    return pl.pallas_call(
        functools.partial(expert_kernel, n_head, n_seq, first, group),
        out_shape=[result(1, F32), result(n_head // 2 - 1, BF16), result(n_head // 2, BF16)],
        in_specs=[pl.BlockSpec(memory_space=pltpu.SMEM)]
        + [whole] * (1 + n_head)
        + [pl.BlockSpec(memory_space=pltpu.HBM)] * 6,
        out_specs=[whole] * 3,
        scratch_shapes=[pltpu.VMEM((rows, width), BF16), pltpu.VMEM((rows, 128), F32)]
        + [pltpu.VMEM((group,) + w.shape[1:], w.dtype) for w in weights[:3]]
        + [pltpu.VMEM(w.shape, w.dtype) for w in weights[3:]]
        + [pltpu.VMEM((rows, width), BF16), pltpu.SemaphoreType.DMA((3, group + 1))],
        cost_estimate=pl.CostEstimate(
            flops=2 * rows * width * (rows + 6 * weights[0].shape[2]),
            transcendentals=rows * weights[0].shape[2],
            bytes_accessed=6 * (group + 1) * width * weights[0].shape[2] + 8 * rows * width,
        ),
        compiler_params=pltpu.CompilerParams(vmem_limit_bytes=SCOPED),
    )(head, regroup, *pieces, *weights)


def shards(
    tokens,
    w_query,
    w_key,
    w_value,
    w_out,
    shared_gate,
    shared_up,
    shared_down,
    expert_gate,
    expert_up,
    expert_down,
    expert_ids,
):
    n_seq, n_head = lax.axis_size("seq"), lax.axis_size("head")
    mine, head = lax.axis_index("seq"), lax.axis_index("head")
    rows, width = tokens.shape
    heads_here = w_query.shape[1] // HD
    experts_here = expert_gate.shape[0]
    part = rows // n_head
    cols = width // n_head
    slots = -(-CAP // n_head)
    chunks = min(CHUNKS, experts_here)
    group = experts_here // chunks

    ids = expert_ids[:, 0]
    order = jnp.arange(rows, dtype=jnp.int32)
    start = jnp.sum((ids[None, :] < ids[:, None]).astype(jnp.int32), axis=1)
    earlier = (ids[None, :] == ids[:, None]) & (order[None, :] < order[:, None])
    rank = jnp.sum(earlier.astype(jnp.int32), axis=1)
    place = start + rank
    quarter = place % n_head
    rel = bit_reverse(quarter ^ head, n_head)
    row = rel * part + place // n_head
    here = order[:, None] == row[None, :]
    deal = here.astype(BF16)
    came_from = jnp.sum(jnp.where(here, order[None, :], 0), axis=1)
    slot = rank // n_head
    owner = (ids // experts_here) ^ mine
    local = ids % experts_here
    half = n_seq // 2

    def place_in(inner, size):
        near = (owner * chunks + local // group) * size
        far = (half * chunks + (local // group) * half + owner - half) * size
        return jnp.where(owner < half, near, far) + inner

    sent_rows, back_size = group * slots, group * slots * n_head
    cell = place_in((local % group) * slots + slot, sent_rows)
    own_cell = jnp.sum(jnp.where(here[:part], cell[None, :], 0), axis=1)
    pack = one_hot(own_cell, n_seq * chunks * sent_rows)
    back_row = place_in(((local % group) * n_head + quarter) * slots + slot, back_size)
    unpack = (
        back_row[:, None] == jnp.arange(n_seq * chunks * back_size, dtype=jnp.int32)[None, :]
    ).astype(BF16)

    chunk_rows = n_head * n_seq * group * slots
    at = jnp.arange(chunk_rows, dtype=jnp.int32)
    at_slot, at_expert = at % slots, (at // slots) % group
    at_seq = (at // (slots * group)) % n_seq
    at_head = bit_reverse(at // (slots * group * n_seq), n_head) ^ head
    regroup = one_hot(
        ((at_expert * n_seq + at_seq) * n_head + at_head) * slots + at_slot, chunk_rows
    )
    head_index = jnp.reshape(head, (1,)).astype(jnp.int32)

    inputs = tokens.astype(F32)
    scale = lax.rsqrt(jnp.mean(inputs * inputs, axis=-1, keepdims=True) + EPS)

    def project(weights, scale):
        return (jnp.dot(tokens, weights, preferred_element_type=F32) * scale).astype(BF16)

    key_rows = project(w_key, scale).reshape(rows, heads_here, HD)
    value_rows = project(w_value, scale).reshape(rows, heads_here, HD)
    state = jnp.einsum("thd,the->hde", key_rows, value_rows, preferred_element_type=F32)
    carried, first = exclusive_sum(state)
    carried = carried.astype(BF16)
    scale, _ = lax.optimization_barrier((scale, first))
    query_rows = jnp.dot(deal, project(w_query, scale), preferred_element_type=F32)
    query_rows = query_rows.astype(BF16).reshape(rows, heads_here, HD)
    scores = jnp.einsum("thd,shd->hts", query_rows, key_rows, preferred_element_type=F32)
    causal = came_from[:, None] >= order[None, :]
    scores = jnp.where(causal[None], scores, 0.0).astype(BF16)
    within = jnp.einsum("hts,shd->htd", scores, value_rows, preferred_element_type=F32)
    keep, send = attention_out(
        query_rows.reshape(rows, heads_here * HD),
        carried,
        within,
        w_out,
    )
    own_tokens = dot(deal[:part], tokens).astype(BF16)
    partial, got = fold(keep, send)

    weights = (expert_gate, expert_up, expert_down, shared_gate, shared_up, shared_down)
    outgoing = pack_rows(pack, own_tokens, partial, got)
    near, far = unstack(outgoing, half, chunks, sent_rows)
    near = [near[0]] + [swap(near[k], "seq", k) for k in range(1, half)]
    far = [[swap(far[c][k], "seq", half + k) for k in range(half)] for c in range(chunks)]
    totals = []
    done = None
    for c in range(chunks):
        blocks = [block[c * sent_rows : (c + 1) * sent_rows] for block in near] + far[c]
        pieces = gather(jnp.concatenate(blocks), done)
        own, rest, other = experts(head_index, regroup, pieces, c * group, group, weights, n_seq)
        done = own
        total = fold_columns(own, rest, other, totals).astype(BF16)
        totals.append(total.reshape(n_seq, back_size, cols))
    back = [jnp.concatenate([total[k] for total in totals]) for k in range(half)]
    far = [[swap(total[k], "seq", k) for k in range(half, n_seq)] for total in totals]
    tied = lax.optimization_barrier((*back[1:], *far[0]))
    back = back[:1] + [swap(tied[k], "seq", k + 1) for k in range(half - 1)]
    back = back + list(tied[half - 1 :]) + [one for blocks in far[1:] for one in blocks]
    result = dot(unpack, jnp.concatenate(back))
    return result.astype(BF16)


def solution(mesh):
    return jax.shard_map(
        shards,
        mesh=mesh,
        in_specs=(
            P("seq", None),
            P(None, "head"),
            P(None, "head"),
            P(None, "head"),
            P("head", None),
            P(None, "head"),
            P(None, "head"),
            P("head", None),
            P("seq", None, "head"),
            P("seq", None, "head"),
            P("seq", "head", None),
            P("seq", None),
        ),
        out_specs=P("seq", "head"),
        check_vma=False,
    )
```
